32 devices in a mesh: group: 4 (over y, x), member: 8 (over z, core).
Axes of the slice: x: 2, y: 2, z: 4, core: 2. Of those that a mesh axis runs over, the one named last changes fastest.
Arguments:
- old_ids: int32 [512], P(('group', 'member')), may hold values from -1 to 255, as said below
- field_old: float32 [512, 32, 1024], P(('group', 'member')), may hold values from -6 to 6
- source_old: float32 [512, 32, 1024], P(('group', 'member')), may hold values from -12 to 12
- kappa_old: float32 [512, 32, 1024], P(('group', 'member')), may hold values from 0.5 to 5
- refine: int32 [256], P(('group', 'member')), may hold values 0 or 1
- neighbors: int32 [256, 6], P(('group', 'member')), may hold values from -1 to 255, as said below
- coarse_inverse: float32 [4, 512, 512], P('group', 'member'), may hold values from -0.0546875 to 0.0546875
Outputs:
- solution: float32 [256, 32, 1024], P(('group', 'member'))
The draws below stay inside these ranges and needn't reach their ends.
Inputs may be any that keep to these rules, and one draw needn't show every extreme that they name: `old_ids`: on each device the live slots come first and hold consecutive curve indices in increasing order, devices following one another along the curve; every block's new owner (index // 8) is the device that holds it or the next one; some device fills all 16 slots. Blocks form a grid in Morton order (bit i of a curve index is a bit of coordinate i mod 3); neighbors[g, k] is either -1 or the block adjacent to g across face k in that grid; relations are mutual: neighbors[g, k] = h means neighbors[h, k xor 1] = g.
All inputs are finite; a program needn't handle non-finite values. No bound on the sum of `refine` on one device may be relied on, other than what follows from the above.
Results may differ from the reference program's by a relative error of at most 0.000078.
Values sent between devices are 32-bit elements; how exact they have to be, the bound alone decides.
A program may use at most 128 MiB of HBM per device.

```python
import math
import jax
import jax.numpy as jnp
from jax import lax

NB = 8
EDGE = 32
OLDCAP = 16
NBLK = 256
CG = 512
N_GROUP = 4
DEVICES = 32


def draw_old_ids(key, part):
    devices_all = NBLK // NB
    position = jnp.arange(devices_all + 1, dtype=jnp.int32)
    extra = jax.random.randint(key, (devices_all + 1,), 0, NB + 1).astype(jnp.int32)
    extra = jnp.where(position == 1, NB, extra)
    extra = jnp.where(position == devices_all - 1, NB, extra)
    extra = jnp.where(position == 0, 0, extra)
    extra = jnp.where(position == devices_all, 0, extra)
    starts = position * NB + extra
    counts = starts[1:] - starts[:-1]
    slot_ids = jnp.arange(2 * NB, dtype=jnp.int32)
    block_ids = starts[:-1, None] + slot_ids[None, :]
    return jnp.where(slot_ids[None, :] < counts[:, None], block_ids, -1).reshape(-1).astype(jnp.int32)


def decode_bits(block_ids, nbits):
    coords = [jnp.zeros_like(block_ids), jnp.zeros_like(block_ids), jnp.zeros_like(block_ids)]
    for bit_id in range(nbits):
        coords[bit_id % 3] = coords[bit_id % 3] + block_ids // 2 ** bit_id % 2 * 2 ** (bit_id // 3)
    return coords


def encode_bits(coords, nbits):
    result = jnp.zeros_like(coords[0])
    for bit_id in range(nbits):
        result = result + coords[bit_id % 3] // 2 ** (bit_id // 3) % 2 * 2 ** bit_id
    return result


def draw_neighbors(key, part):
    nbits = NBLK.bit_length() - 1
    block_ids = jnp.arange(NBLK, dtype=jnp.int32)
    coords = decode_bits(block_ids, nbits)
    extents = [2 ** len([bit_id for bit_id in range(nbits) if bit_id % 3 == axis_id]) for axis_id in range(3)]
    cut_plus = jax.random.randint(key, (NBLK, 3), 0, 8).astype(jnp.int32) == 0
    columns = []
    for axis_id in range(3):
        for step_sign in (-1, 1):
            moved = coords[axis_id] + step_sign
            inside = jnp.logical_and(moved >= 0, moved < extents[axis_id])
            new_coords = list(coords)
            new_coords[axis_id] = jnp.clip(moved, 0, extents[axis_id] - 1)
            target = encode_bits(new_coords, nbits)
            if step_sign == 1:
                cut_face = cut_plus[:, axis_id]
            else:
                cut_face = cut_plus[target, axis_id]
            columns.append(jnp.where(jnp.logical_and(inside, jnp.logical_not(cut_face)), target, -1))
    return jnp.stack(columns, axis=1).astype(jnp.int32)


def plant(drawn, rng, low, top_value):
    longest = drawn.shape.index(max(drawn.shape))
    spots = []
    for shift in (0, 1):
        where = [jax.random.randint(jax.random.fold_in(rng, axis), (), 0, length) for axis, length in enumerate(drawn.shape)]
        where[longest] = (where[longest] + shift) % drawn.shape[longest]
        spots.append(tuple(where))
    return drawn.at[spots[0]].set(low).at[spots[1]].set(top_value)


def block_scale(rng, shape, split, low, top_value):
    gain = 1.0
    for axis_at, parts in split:
        heights = jax.random.uniform(jax.random.fold_in(jax.random.fold_in(rng, 6), axis_at), (parts,), jnp.float32, low / len(split), top_value / len(split))
        gain = gain * jnp.repeat(jnp.exp(heights), shape[axis_at] // parts).reshape((-1,) + (1,) * (len(shape) - 1 - axis_at))
    return gain


def centred(stream_key, shape, width, bound, pieces=(), kind=jnp.bfloat16):
    values = width * jax.random.normal(stream_key, shape, jnp.float32)
    if pieces:
        values = values * block_scale(stream_key, shape, pieces, -0.22, 0.18)
    return jnp.clip(values, -bound, bound).astype(kind)


def setup_inputs(seed: int = 0) -> dict:
    splits = jax.random.split(jax.random.key(seed), 8)
    return {
        "old_ids": draw_old_ids(jax.random.fold_in(splits[7], 71), 0),
        "field_old": centred(splits[1], (DEVICES * OLDCAP, EDGE, EDGE * EDGE), 1.0, 6.0, ((0, 32),), jnp.float32),
        "source_old": centred(splits[2], (DEVICES * OLDCAP, EDGE, EDGE * EDGE), 2.0, 12.0, ((0, 32),), jnp.float32),
        "kappa_old": jnp.clip(jnp.exp(math.log(5.0) - 2.3025851 * jax.random.uniform(splits[3], (DEVICES * OLDCAP, EDGE, EDGE * EDGE), jnp.float32) ** block_scale(splits[3], (DEVICES * OLDCAP, EDGE, EDGE * EDGE), ((0, 32),), -0.2, 0.2)), 0.5, 5.0),
        "refine": plant((jax.random.randint(splits[4], (NBLK,), 0, 2) < 1).astype(jnp.int32), jax.random.fold_in(splits[4], 1), 0, 1),
        "neighbors": draw_neighbors(jax.random.fold_in(splits[7], 71), 0),
        "coarse_inverse": centred(splits[6], (N_GROUP, CG, CG), (25 * CG) ** -0.5, 0.0546875, ((0, 4), (1, 8)), jnp.float32),
    }


OMEGA = 0.8
OPPOSITE = (1, 0, 3, 2, 5, 4)


def face_layers(volume):
    blocks, edge_cells, face_cells = volume.shape
    cube_view = volume.reshape(blocks, edge_cells, edge_cells, edge_cells)
    planes = [cube_view[:, 0], cube_view[:, edge_cells - 1], cube_view[:, :, 0], cube_view[:, :, edge_cells - 1], cube_view[:, :, :, 0], cube_view[:, :, :, edge_cells - 1]]
    return jnp.stack([plane_one.reshape(blocks, face_cells) for plane_one in planes], axis=1)


def beside(values, ghosts):
    blocks, edge_cells, face_cells = values.shape
    sheets = ghosts.reshape(blocks, 6, edge_cells, edge_cells)
    x_minus = jnp.concatenate([ghosts[:, 0][:, None, :], values[:, :-1]], axis=1)
    x_plus = jnp.concatenate([values[:, 1:], ghosts[:, 1][:, None, :]], axis=1)
    y_minus = jnp.concatenate([sheets[:, 2], values[:, :, :-edge_cells]], axis=2)
    y_plus = jnp.concatenate([values[:, :, edge_cells:], sheets[:, 3]], axis=2)
    depth = lax.iota(jnp.int32, face_cells) % edge_cells
    zero_col = jnp.zeros_like(values[:, :, :1])
    z_minus = jnp.where(depth == 0, jnp.repeat(sheets[:, 4], edge_cells, axis=2), jnp.concatenate([zero_col, values[:, :, :-1]], axis=2))
    z_plus = jnp.where(depth == edge_cells - 1, jnp.repeat(sheets[:, 5], edge_cells, axis=2), jnp.concatenate([values[:, :, 1:], zero_col], axis=2))
    return [x_minus, x_plus, y_minus, y_plus, z_minus, z_plus]


def face_weights(kappa, kappa_ghosts, inv_spacing):
    return [inv_spacing * (0.5 * (kappa + across)) for across in beside(kappa, kappa_ghosts)]


def smooth_terms(values, ghosts, weights):
    applied = jnp.zeros_like(values)
    diagonal = jnp.zeros_like(values)
    for weight, across in zip(weights, beside(values, ghosts)):
        applied = applied + weight * (values - across)
        diagonal = diagonal + weight
    return applied, diagonal


def restrict(residual):
    blocks, edge_cells, face_cells = residual.shape
    half_edge = edge_cells // 2
    split_view = residual.reshape(blocks, 2, half_edge, 2, half_edge, 2, half_edge)
    return jnp.sum(split_view, axis=(2, 4, 6)).reshape(blocks * 8) * (half_edge ** -1.5)


def prolong(values, correction):
    blocks, edge_cells, face_cells = values.shape
    half_edge = edge_cells // 2
    split_view = values.reshape(blocks, 2, half_edge, 2, half_edge, 2, half_edge)
    lifted = correction.reshape(blocks, 2, 1, 2, 1, 2, 1)
    return (split_view + lifted).reshape(values.shape)


def reference(old_ids, field_old, source_old, kappa_old, refine, neighbors, coarse_inverse):
    places = jnp.where(old_ids >= 0, old_ids, NBLK).astype(jnp.int32)

    def settle(old_values):
        empty_set = jnp.zeros((NBLK + 1,) + old_values.shape[1:], jnp.float32)
        return empty_set.at[places].set(old_values)[:NBLK]

    field_new = settle(field_old)
    source = settle(source_old)
    kappa = settle(kappa_old)
    inv_spacing = (1.0 + refine.astype(jnp.float32))[:, None, None]
    opposite = jnp.array(OPPOSITE, jnp.int32)
    has_side = (neighbors >= 0)[:, :, None]
    source_rows = jnp.maximum(neighbors, 0).astype(jnp.int32)

    def ghosts_of(values):
        sheets = face_layers(values)
        return jnp.where(has_side, sheets[source_rows, opposite[None, :]], 0.0)

    kappa_ghosts = jnp.where(has_side, ghosts_of(kappa), face_layers(kappa))
    weights = face_weights(kappa, kappa_ghosts, inv_spacing)
    for sweep_id in range(2):
        applied, diagonal = smooth_terms(field_new, ghosts_of(field_new), weights)
        field_new = field_new + OMEGA * (source - applied) / diagonal
    applied, diagonal = smooth_terms(field_new, ghosts_of(field_new), weights)
    coarse = restrict(source - applied).reshape(N_GROUP, CG)
    correction = jnp.einsum("gij,gj->gi", coarse_inverse, coarse, precision=lax.Precision.HIGHEST)
    return prolong(field_new, correction.reshape(NBLK * 8))
```

```python
import functools

import jax
import jax.numpy as jnp
from jax import lax
from jax.experimental import pallas as pl
from jax.experimental.pallas import tpu as pltpu
from jax.sharding import PartitionSpec as P

OMEGA = 0.8
AXES = ("group", "member")
NB, EDGE, FACE = 8, 32, 1024
HIGHEST = lax.Precision.HIGHEST
VMEM_LIMIT = 40 * 2**20
VM = pl.BlockSpec(memory_space=pltpu.VMEM)
SM = pl.BlockSpec(memory_space=pltpu.SMEM)
FACE_SHAPES = ((4, FACE), (EDGE, 128), (8, FACE))


def roll(value, steps):
    width = value.shape[-1]
    return pltpu.roll(value, steps % width, value.ndim - 1)


def depth_lanes(shape):
    return lax.broadcasted_iota(jnp.int32, shape, len(shape) - 1) % EDGE


def blocks_of(axis, side):
    return [b for b in range(NB) if (b >> axis) % 2 == side]


def pack_faces(load, outs):
    segment = lax.broadcasted_iota(jnp.int32, (EDGE, 128), 1) // EDGE
    depth = depth_lanes((8, FACE))
    everything = slice(0, FACE)
    for side in (0, 1):
        for j, b in enumerate(blocks_of(0, side)):
            row = (EDGE - 1) * side
            outs[0][side][j : j + 1, :] = load(b, slice(row, row + 1), everything)
        packed = jnp.zeros((EDGE, 128), jnp.float32)
        for j, b in enumerate(blocks_of(1, side)):
            low = (FACE - 128) * side
            piece = load(b, slice(0, EDGE), slice(low, low + 128))
            packed = jnp.where(segment == j, roll(piece, EDGE * (j - 3 * side)), packed)
        outs[1][side][...] = packed
        packed = jnp.zeros((8, FACE), jnp.float32)
        for j, b in enumerate(blocks_of(2, side)):
            for part in range(4):
                slot = 4 * j + part
                piece = load(b, slice(8 * part, 8 * part + 8), everything)
                packed = jnp.where(depth == slot, roll(piece, slot - 31 * side), packed)
        outs[2][side][...] = packed


def fill(values, ghosts, nbrs, pad, sheet, mirror):
    everything = slice(0, FACE)
    depth = depth_lanes((8, FACE))
    for b in range(NB):
        pad[b, 8:40, 128 : 128 + FACE] = values[b]
        for side in (0, 1):
            inside = [(b >> axis) % 2 != side for axis in range(3)]
            has = [nbrs[b, 2 * axis + side] >= 0 for axis in range(3)]
            j = [blocks_of(a, side).index(b) if not inside[a] else 0 for a in range(3)]
            row, far = (EDGE - 1) * side, (EDGE - 1) * (1 - side)
            if inside[0]:
                ghost = values[b ^ 1, far : far + 1, :]
            else:
                ghost = ghosts[0][side][j[0] : j[0] + 1, :]
            spare = values[b, row : row + 1, :] if mirror else jnp.zeros_like(ghost)
            place = 7 + 33 * side
            pad[b, place : place + 1, 128 : 128 + FACE] = jnp.where(has[0], ghost, spare)
            low, high = (FACE - 128) * side, (FACE - 128) * (1 - side)
            if inside[1]:
                ghost = values[b ^ 2, :, high : high + 128]
            else:
                ghost = roll(ghosts[1][side][...], EDGE * (3 * (1 - side) - j[1]))
            if mirror:
                spare = roll(values[b, :, low : low + 128], EDGE * (3 - 6 * side))
            else:
                spare = jnp.zeros_like(ghost)
            place = (128 + FACE) * side
            pad[b, 8:40, place : place + 128] = jnp.where(has[1], ghost, spare)
        for part in range(4):
            rows = slice(8 * part, 8 * part + 8)
            own = values[b, rows, :]
            near = []
            for side in (0, 1):
                if (b >> 2) % 2 != side:
                    ghost = roll(values[b ^ 4, rows, :], 31 * (2 * side - 1))
                else:
                    slot = 4 * blocks_of(2, side).index(b) + part
                    ghost = roll(ghosts[2][side][...], 31 * side - slot)
                spare = own if mirror else jnp.zeros_like(own)
                near.append(jnp.where(nbrs[b, 4 + side] >= 0, ghost, spare))
            sheet[b, rows, :] = jnp.where(depth < EDGE // 2, near[0], near[1])


def across(pad, sheet, b, part):
    depth = depth_lanes((8, FACE))
    top = 8 + 8 * part
    inner = slice(128, 128 + FACE)
    x_minus = pad[b, top - 1 : top + 7, inner]
    x_plus = pad[b, top + 1 : top + 9, inner]
    whole = pad[b, top : top + 8, :]
    edge = sheet[b, 8 * part : 8 * part + 8, :]
    y_minus = roll(whole, EDGE)[:, inner]
    y_plus = roll(whole, -EDGE)[:, inner]
    z_minus = jnp.where(depth == 0, edge, roll(whole, 1)[:, inner])
    z_plus = jnp.where(depth == EDGE - 1, edge, roll(whole, -1)[:, inner])
    return whole[:, inner], (x_minus, x_plus, y_minus, y_plus, z_minus, z_plus)


def terms(pad_u, sheet_u, pad_k, sheet_k, b, part, half_scale):
    u, around_u = across(pad_u, sheet_u, b, part)
    k, around_k = across(pad_k, sheet_k, b, part)
    applied = jnp.zeros_like(u)
    diagonal = jnp.zeros_like(u)
    for other_u, other_k in zip(around_u, around_k):
        weight = k + other_k
        applied = applied + weight * (u - other_u)
        diagonal = diagonal + weight
    return u, half_scale * applied, half_scale * diagonal


def pairs(refs):
    return [refs[2 * axis : 2 * axis + 2] for axis in range(3)]


def merge_kernel(moved, *refs):
    mine, theirs, merged = refs[0:3], refs[3:6], refs[6:9]
    out_u, out_k = pairs(refs[9:15]), pairs(refs[15:21])
    count = moved[0]

    def body(p, carry):
        for own, got, out in zip(mine, theirs, merged):
            out[p] = jnp.where(p < count, got[p], own[jnp.maximum(p - count, 0)])
        return carry

    lax.fori_loop(0, NB, body, 0)
    for values, outs in ((merged[0], out_u), (merged[2], out_k)):
        pack_faces(lambda b, rows, lanes, values=values: values[b, rows, lanes], outs)


def smooth_kernel(last, nbrs, refine, u_ref, f_ref, k_ref, *refs):
    ghosts_u, ghosts_k = pairs(refs[0:6]), pairs(refs[6:12])
    outs = refs[12:-4]
    pad_u, sheet_u, pad_k, sheet_k = refs[-4:]
    fill(u_ref, ghosts_u, nbrs, pad_u, sheet_u, False)
    fill(k_ref, ghosts_k, nbrs, pad_k, sheet_k, True)

    def body(b, carry):
        half_scale = 0.5 + 0.5 * refine[b].astype(jnp.float32)
        total = None
        for part in range(4):
            rows = slice(8 * part, 8 * part + 8)
            u, applied, diagonal = terms(pad_u, sheet_u, pad_k, sheet_k, b, part, half_scale)
            gap = f_ref[b, rows, :] - applied
            if not last:
                outs[0][b, rows, :] = u + OMEGA * gap / diagonal
            else:
                total = gap if part % 2 == 0 else total + gap
                if part % 2 == 1:
                    outs[0][b, part // 2] = total
        return carry

    lax.fori_loop(0, NB, body, 0)
    if not last:
        pack_faces(lambda b, rows, lanes: outs[0][b, rows, lanes], pairs(outs[1:7]))


def finish_kernel(u_ref, rows_ref, out_ref):
    for b in range(NB):
        for part in range(4):
            place = 2 * b + part // 2
            rows = slice(8 * part, 8 * part + 8)
            out_ref[b, rows, :] = u_ref[b, rows, :] + rows_ref[place : place + 1, :]


def face_partners(members, devices):
    here = lax.axis_index("group") * members + lax.axis_index("member")
    nbits = devices.bit_length() - 1
    bits = [here // 2**i % 2 for i in range(nbits)]
    result = []
    for axis in range(3):
        own = [i for i in range(nbits) if i % 3 == axis]
        extent = 2 ** len(own)
        coord = sum(bits[i] * 2**n for n, i in enumerate(own))
        base = here - sum(bits[i] * 2**i for i in own)
        pair = []
        for step in (-1, 1):
            moved = coord + step
            inside = jnp.logical_and(moved >= 0, moved < extent)
            clipped = jnp.clip(moved, 0, extent - 1)
            index = base + sum(clipped // 2**n % 2 * 2**i for n, i in enumerate(own))
            pair.append((inside, (index // members, index % members)))
        result.append(pair)
    return result


def exchange_kernel(members, devices, sets, *refs):
    count = 6 * sets
    sources, targets = refs[:count], refs[count : 2 * count]
    send, recv = refs[2 * count :]
    partners = face_partners(members, devices)
    barrier = pltpu.get_barrier_semaphore()
    present = jnp.int32(0)
    for axis in range(3):
        for side in (0, 1):
            inside, peer = partners[axis][side]
            present = present + inside.astype(jnp.int32)

            @pl.when(inside)
            def _():
                pl.semaphore_signal(
                    barrier, inc=1, device_id=peer, device_id_type=pl.DeviceIdType.MESH
                )

    pl.semaphore_wait(barrier, present)

    def copy_of(group, axis, side, peer):
        out = 6 * group + 2 * axis + side
        into = 6 * group + 2 * axis + 1 - side
        return pltpu.make_async_remote_copy(
            src_ref=sources[out],
            dst_ref=targets[into],
            send_sem=send.at[out],
            recv_sem=recv.at[into],
            device_id=peer,
            device_id_type=pl.DeviceIdType.MESH,
        )

    every = [(g, a, s) for g in range(sets) for a in range(3) for s in (0, 1)]
    for group, axis, side in every:
        inside, peer = partners[axis][side]

        @pl.when(inside)
        def _():
            copy_of(group, axis, side, peer).start()

    for group, axis, side in every:
        inside, peer = partners[axis][side]

        @pl.when(inside)
        def _():
            copy_of(group, axis, side, peer).wait_send()
            copy_of(group, axis, 1 - side, peer).wait_recv()


def exchange(faces, ident):
    sets = len(faces) // 6
    shapes = [jax.ShapeDtypeStruct(f.shape, f.dtype) for f in faces]
    members = lax.axis_size("member")
    devices = lax.axis_size(AXES)
    return pl.pallas_call(
        functools.partial(exchange_kernel, members, devices, sets),
        out_shape=shapes,
        in_specs=[VM] * len(faces),
        out_specs=[VM] * len(faces),
        scratch_shapes=[
            pltpu.SemaphoreType.DMA((len(faces),)),
            pltpu.SemaphoreType.DMA((len(faces),)),
        ],
        compiler_params=pltpu.CompilerParams(collective_id=ident, has_side_effects=True),
    )(*faces)


def gather_kernel(members, mine, out, send, recv, local_sem):
    me = lax.axis_index("member")
    barrier = pltpu.get_barrier_semaphore()
    for step in range(1, members):
        pl.semaphore_signal(
            barrier,
            inc=1,
            device_id={"member": (me + step) % members},
            device_id_type=pl.DeviceIdType.MESH,
        )
    pl.semaphore_wait(barrier, members - 1)

    def copy_of(step):
        return pltpu.make_async_remote_copy(
            src_ref=mine,
            dst_ref=out.at[me],
            send_sem=send.at[step],
            recv_sem=recv.at[step],
            device_id={"member": (me + step) % members},
            device_id_type=pl.DeviceIdType.MESH,
        )

    for step in range(1, members):
        copy_of(step).start()
    out[me] = mine[...]
    for step in range(1, members):
        copy_of(step).wait_send()
        copy_of(step).wait_recv()


def gather(rows, ident):
    members = lax.axis_size("member")
    return pl.pallas_call(
        functools.partial(gather_kernel, members),
        out_shape=jax.ShapeDtypeStruct((members,) + rows.shape, rows.dtype),
        in_specs=[VM],
        out_specs=VM,
        scratch_shapes=[
            pltpu.SemaphoreType.DMA((members,)),
            pltpu.SemaphoreType.DMA((members,)),
            pltpu.SemaphoreType.DMA,
        ],
        compiler_params=pltpu.CompilerParams(collective_id=ident, has_side_effects=True),
    )(rows)


def face_structs():
    return [jax.ShapeDtypeStruct(s, jnp.float32) for s in FACE_SHAPES for _ in (0, 1)]


def smooth(last, nbrs, refine, u, f, k, ghosts_u, ghosts_k):
    if last:
        outs = [jax.ShapeDtypeStruct((NB, 2, 8, FACE), jnp.float32)]
    else:
        outs = [jax.ShapeDtypeStruct(u.shape, jnp.float32)] + face_structs()
    return pl.pallas_call(
        functools.partial(smooth_kernel, last),
        out_shape=outs,
        in_specs=[SM, SM] + [VM] * 15,
        out_specs=[VM] * len(outs),
        scratch_shapes=[
            pltpu.VMEM((NB, 48, FACE + 256), jnp.float32),
            pltpu.VMEM((NB, EDGE, FACE), jnp.float32),
            pltpu.VMEM((NB, 48, FACE + 256), jnp.float32),
            pltpu.VMEM((NB, EDGE, FACE), jnp.float32),
        ],
        compiler_params=pltpu.CompilerParams(vmem_limit_bytes=VMEM_LIMIT),
    )(nbrs, refine, u, f, k, *ghosts_u, *ghosts_k)


def local(old_ids, field_old, source_old, kappa_old, refine, neighbors, coarse_inverse):
    devices = lax.axis_size(AXES)
    here = lax.axis_index(AXES)
    kept = jnp.sum(
        jnp.logical_and(old_ids >= 0, old_ids // NB == here).astype(jnp.int32), dtype=jnp.int32
    )
    olds = (field_old, source_old, kappa_old)
    leaving = [lax.dynamic_slice_in_dim(a, kept, NB, 0) for a in olds]
    arrived = lax.ppermute(leaving, AXES, [(i, i + 1) for i in range(devices - 1)])
    block = pl.BlockSpec((NB, EDGE, FACE), lambda i: (0, 0, 0))
    whole = jax.ShapeDtypeStruct((NB, EDGE, FACE), jnp.float32)
    small = [pl.BlockSpec(s, lambda i: (0, 0)) for s in FACE_SHAPES for _ in (0, 1)]
    merged = pl.pallas_call(
        merge_kernel,
        grid=(1,),
        out_shape=[whole] * 3 + face_structs() * 2,
        in_specs=[SM] + [block] * 6,
        out_specs=[block] * 3 + small * 2,
        compiler_params=pltpu.CompilerParams(vmem_limit_bytes=VMEM_LIMIT),
    )((NB - kept)[None], *olds, *arrived)
    u, f, k = merged[:3]
    ghosts = exchange(merged[3:], 1)
    ghosts_u, ghosts_k = ghosts[:6], ghosts[6:]
    for sweep in range(2):
        u, *faces = smooth(False, neighbors, refine, u, f, k, ghosts_u, ghosts_k)
        ghosts_u = exchange(faces, 2 + sweep)
    (sums,) = smooth(True, neighbors, refine, u, f, k, ghosts_u, ghosts_k)
    lanes = lax.iota(jnp.int32, FACE)
    cell = lanes // (FACE // 2) * 2 + lanes % EDGE // (EDGE // 2)
    choose = (cell[:, None] == lax.iota(jnp.int32, 128)[None, :]).astype(jnp.float32)
    rows = jnp.sum(sums, axis=2).reshape(2 * NB, FACE)
    coarse = jnp.dot(rows, choose, precision=HIGHEST) * (EDGE // 2) ** (-1.5)
    gathered = gather(coarse, 4)[:, :, :4].reshape(-1)
    e = jnp.dot(coarse_inverse[0], gathered, precision=HIGHEST)
    lifted = jnp.broadcast_to(
        e.reshape(2 * NB, 2, 1, 2, 1), (2 * NB, 2, EDGE // 2, 2, EDGE // 2)
    ).reshape(2 * NB, FACE)
    return pl.pallas_call(
        finish_kernel,
        out_shape=whole,
        in_specs=[VM, VM],
        out_specs=VM,
        compiler_params=pltpu.CompilerParams(vmem_limit_bytes=VMEM_LIMIT),
    )(u, lifted)


def solution(mesh):
    in_specs = (
        P(AXES),
        P(AXES, None, None),
        P(AXES, None, None),
        P(AXES, None, None),
        P(AXES),
        P(AXES, None),
        P("group", "member", None),
    )
    return jax.shard_map(
        local, mesh=mesh, in_specs=in_specs, out_specs=P(AXES, None, None), check_vma=False
    )
```

```python
import functools

import jax
import jax.numpy as jnp
from jax import lax
from jax.experimental import pallas as pl
from jax.experimental.pallas import tpu as pltpu
from jax.sharding import PartitionSpec as P

OMEGA = 0.8
AXES = ("group", "member")
NB, EDGE, FACE = 8, 32, 1024
HIGHEST = lax.Precision.HIGHEST
VMEM_LIMIT = 56 * 2**20
VM = pl.BlockSpec(memory_space=pltpu.VMEM)
ANY = pl.BlockSpec(memory_space=pl.ANY)
MESH = pl.DeviceIdType.MESH
SM = pl.BlockSpec(memory_space=pltpu.SMEM)
FACE_SHAPES = ((4, FACE), (EDGE, 128), (8, FACE))


def roll(value, steps):
    width = value.shape[-1]
    return pltpu.roll(value, steps % width, value.ndim - 1)


def depth_lanes(shape):
    return lax.broadcasted_iota(jnp.int32, shape, len(shape) - 1) % EDGE


def blocks_of(axis, side):
    return [b for b in range(NB) if (b >> axis) % 2 == side]


def pack_faces(load, outs):
    segment = lax.broadcasted_iota(jnp.int32, (EDGE, 128), 1) // EDGE
    depth = depth_lanes((8, FACE))
    everything = slice(0, FACE)
    for side in (0, 1):
        for j, b in enumerate(blocks_of(0, side)):
            row = (EDGE - 1) * side
            outs[0][side][j : j + 1, :] = load(b, slice(row, row + 1), everything)
        packed = jnp.zeros((EDGE, 128), jnp.float32)
        for j, b in enumerate(blocks_of(1, side)):
            low = (FACE - 128) * side
            piece = load(b, slice(0, EDGE), slice(low, low + 128))
            packed = jnp.where(segment == j, roll(piece, EDGE * (j - 3 * side)), packed)
        outs[1][side][...] = packed
        packed = jnp.zeros((8, FACE), jnp.float32)
        for j, b in enumerate(blocks_of(2, side)):
            for part in range(4):
                slot = 4 * j + part
                piece = load(b, slice(8 * part, 8 * part + 8), everything)
                packed = jnp.where(depth == slot, roll(piece, slot - 31 * side), packed)
        outs[2][side][...] = packed


def fill(values, ghosts, nbrs, pad, sheet, mirror):
    everything = slice(0, FACE)
    depth = depth_lanes((8, FACE))
    for b in range(NB):
        pad[b, 8:40, 128 : 128 + FACE] = values[b]
        for side in (0, 1):
            inside = [(b >> axis) % 2 != side for axis in range(3)]
            has = [nbrs[b, 2 * axis + side] >= 0 for axis in range(3)]
            j = [blocks_of(a, side).index(b) if not inside[a] else 0 for a in range(3)]
            row, far = (EDGE - 1) * side, (EDGE - 1) * (1 - side)
            if inside[0]:
                ghost = values[b ^ 1, far : far + 1, :]
            else:
                ghost = ghosts[0][side][j[0] : j[0] + 1, :]
            spare = values[b, row : row + 1, :] if mirror else jnp.zeros_like(ghost)
            place = 7 + 33 * side
            pad[b, place : place + 1, 128 : 128 + FACE] = jnp.where(has[0], ghost, spare)
            low, high = (FACE - 128) * side, (FACE - 128) * (1 - side)
            if inside[1]:
                ghost = values[b ^ 2, :, high : high + 128]
            else:
                ghost = roll(ghosts[1][side][...], EDGE * (3 * (1 - side) - j[1]))
            if mirror:
                spare = roll(values[b, :, low : low + 128], EDGE * (3 - 6 * side))
            else:
                spare = jnp.zeros_like(ghost)
            place = (128 + FACE) * side
            pad[b, 8:40, place : place + 128] = jnp.where(has[1], ghost, spare)
        for part in range(4):
            rows = slice(8 * part, 8 * part + 8)
            own = values[b, rows, :]
            near = []
            for side in (0, 1):
                if (b >> 2) % 2 != side:
                    ghost = roll(values[b ^ 4, rows, :], 31 * (2 * side - 1))
                else:
                    slot = 4 * blocks_of(2, side).index(b) + part
                    ghost = roll(ghosts[2][side][...], 31 * side - slot)
                spare = own if mirror else jnp.zeros_like(own)
                near.append(jnp.where(nbrs[b, 4 + side] >= 0, ghost, spare))
            sheet[b, rows, :] = jnp.where(depth < EDGE // 2, near[0], near[1])


def across(pad, sheet, b, part):
    depth = depth_lanes((8, FACE))
    top = 8 + 8 * part
    inner = slice(128, 128 + FACE)
    x_minus = pad[b, top - 1 : top + 7, inner]
    x_plus = pad[b, top + 1 : top + 9, inner]
    whole = pad[b, top : top + 8, :]
    edge = sheet[b, 8 * part : 8 * part + 8, :]
    y_minus = roll(whole, EDGE)[:, inner]
    y_plus = roll(whole, -EDGE)[:, inner]
    z_minus = jnp.where(depth == 0, edge, roll(whole, 1)[:, inner])
    z_plus = jnp.where(depth == EDGE - 1, edge, roll(whole, -1)[:, inner])
    return whole[:, inner], (x_minus, x_plus, y_minus, y_plus, z_minus, z_plus)


def face_partners(members, devices):
    here = lax.axis_index("group") * members + lax.axis_index("member")
    nbits = devices.bit_length() - 1
    bits = [here // 2**i % 2 for i in range(nbits)]
    result = []
    for axis in range(3):
        own = [i for i in range(nbits) if i % 3 == axis]
        extent = 2 ** len(own)
        coord = sum(bits[i] * 2**n for n, i in enumerate(own))
        base = here - sum(bits[i] * 2**i for i in own)
        pair = []
        for step in (-1, 1):
            moved = coord + step
            inside = jnp.logical_and(moved >= 0, moved < extent)
            clipped = jnp.clip(moved, 0, extent - 1)
            index = base + sum(clipped // 2**n % 2 * 2**i for n, i in enumerate(own))
            pair.append((inside, (index // members, index % members)))
        result.append(pair)
    return result


def main_kernel(
    members, devices, old_ids, nbrs, refine, inverse, u_old, f_old, k_old, out_ref, *scratch
):
    olds, stages, gots = scratch[0:3], scratch[3:6], scratch[6:9]
    u_ref, f_ref, k_ref, pad_u, sheet_u, pad_k, sheet_k, weights, sums, mine, all_sums = scratch[9:20]
    sent, ghost = [], []
    for phase in range(4):
        base = 20 + 6 * phase
        sent.append([[r.at[0], r.at[1]] for r in scratch[base : base + 3]])
        ghost.append([[r.at[0], r.at[1]] for r in scratch[base + 3 : base + 6]])
    in_sem, move_send, move_recv, face_send, face_recv, sum_send, sum_recv = scratch[44:51]

    member = lax.axis_index("member")
    here = lax.axis_index("group") * members + member
    partners = face_partners(members, devices)
    has_next, has_prev = here < devices - 1, here > 0
    after = jnp.minimum(here + 1, devices - 1)
    before = jnp.maximum(here - 1, 0)
    after = (after // members, after % members)
    before = (before // members, before % members)

    order = (0, 2, 1)
    loads = [
        pltpu.make_async_copy(ref, olds[i], in_sem.at[i])
        for i, ref in enumerate((u_old, f_old, k_old))
    ]
    for i in order:
        loads[i].start()

    barrier = pltpu.get_barrier_semaphore()
    expected = has_next.astype(jnp.int32) + (members - 1)
    for axis in range(3):
        for side in (0, 1):
            inside, peer = partners[axis][side]
            expected = expected + inside.astype(jnp.int32)

            @pl.when(inside)
            def _():
                pl.semaphore_signal(barrier, inc=1, device_id=peer, device_id_type=MESH)

    for step in range(1, members):
        pl.semaphore_signal(
            barrier,
            inc=1,
            device_id={"member": (member + step) % members},
            device_id_type=MESH,
        )

    @pl.when(has_prev)
    def _():
        pl.semaphore_signal(barrier, inc=1, device_id=before, device_id_type=MESH)

    kept = jnp.int32(0)
    for slot in range(2 * NB):
        index = old_ids[slot]
        own = jnp.logical_and(index >= here * NB, index < here * NB + NB)
        kept = kept + own.astype(jnp.int32)
    kept = jnp.minimum(kept, NB)
    count = NB - kept

    moves = [
        pltpu.make_async_remote_copy(
            src_ref=stages[i],
            dst_ref=gots[i],
            send_sem=move_send.at[i],
            recv_sem=move_recv.at[i],
            device_id=after,
            device_id_type=MESH,
        )
        for i in range(3)
    ]
    for i in order:
        loads[i].wait()

        def stage(p, carry, i=i):
            stages[i][p] = olds[i][kept + p]
            return carry

        lax.fori_loop(0, NB, stage, 0)
        if i == 0:
            pl.semaphore_wait(barrier, expected)

        @pl.when(has_next)
        def _():
            moves[i].start()

    def settle(i, out):
        @pl.when(has_prev)
        def _():
            moves[i].wait_recv()

        def body(p, carry):
            out[p] = jnp.where(p < count, gots[i][p], olds[i][jnp.maximum(p - count, 0)])
            return carry

        lax.fori_loop(0, NB, body, 0)

    def face_copy(phase, axis, side, peer):
        return pltpu.make_async_remote_copy(
            src_ref=sent[phase][axis][side],
            dst_ref=ghost[phase][axis][1 - side],
            send_sem=face_send.at[phase, 2 * axis + side],
            recv_sem=face_recv.at[phase, 2 * axis + 1 - side],
            device_id=peer,
            device_id_type=MESH,
        )

    def send_faces(phase, values):
        pack_faces(lambda b, rows, lanes: values[b, rows, lanes], sent[phase])
        for axis in range(3):
            for side in (0, 1):
                inside, peer = partners[axis][side]

                @pl.when(inside)
                def _():
                    face_copy(phase, axis, side, peer).start()

    def take_faces(phase):
        for axis in range(3):
            for side in (0, 1):
                inside, peer = partners[axis][side]

                @pl.when(inside)
                def _():
                    face_copy(phase, axis, side, peer).wait_send()
                    face_copy(phase, axis, 1 - side, peer).wait_recv()

    settle(0, u_ref)
    send_faces(0, u_ref)
    settle(2, k_ref)
    send_faces(3, k_ref)
    take_faces(0)
    fill(u_ref, ghost[0], nbrs, pad_u, sheet_u, False)
    take_faces(3)
    fill(k_ref, ghost[3], nbrs, pad_k, sheet_k, True)

    def weigh(b, carry):
        half_scale = 0.5 + 0.5 * refine[b].astype(jnp.float32)
        for part in range(4):
            rows = slice(8 * part, 8 * part + 8)
            k, around = across(pad_k, sheet_k, b, part)
            for face in range(6):
                weights[b, face, rows, :] = half_scale * (k + around[face])
        return carry

    lax.fori_loop(0, NB, weigh, 0)
    settle(1, f_ref)

    def terms(b, part, with_diagonal):
        rows = slice(8 * part, 8 * part + 8)
        u, around = across(pad_u, sheet_u, b, part)
        applied = jnp.zeros_like(u)
        diagonal = jnp.zeros_like(u)
        for face in range(6):
            weight = weights[b, face, rows, :]
            applied = applied + weight * (u - around[face])
            if with_diagonal:
                diagonal = diagonal + weight
        return u, f_ref[b, rows, :] - applied, diagonal

    def sweep(b, carry):
        for part in range(4):
            u, gap, diagonal = terms(b, part, True)
            u_ref[b, 8 * part : 8 * part + 8, :] = u + OMEGA * gap / diagonal
        return carry

    for phase in (1, 2):
        lax.fori_loop(0, NB, sweep, 0)
        send_faces(phase, u_ref)
        take_faces(phase)
        fill(u_ref, ghost[phase], nbrs, pad_u, sheet_u, False)

    def residual(b, carry):
        for half in (0, 1):
            gap = terms(b, 2 * half, False)[1] + terms(b, 2 * half + 1, False)[1]
            sums[2 * b + half] = gap
        return carry

    lax.fori_loop(0, NB, residual, 0)

    def cell_of(lane):
        return lane // (FACE // 2) * 2 + lane % EDGE // (EDGE // 2)

    choose = cell_of(lax.broadcasted_iota(jnp.int32, (FACE, 128), 0)) == lax.broadcasted_iota(
        jnp.int32, (FACE, 128), 1
    )
    rows = jnp.sum(sums[...], axis=1)
    mine[...] = jnp.dot(
        rows, choose.astype(jnp.float32), precision=HIGHEST, preferred_element_type=jnp.float32
    ) * (EDGE // 2) ** (-1.5)

    def sum_copy(step):
        return pltpu.make_async_remote_copy(
            src_ref=mine,
            dst_ref=all_sums.at[member],
            send_sem=sum_send.at[step],
            recv_sem=sum_recv.at[step],
            device_id={"member": (member + step) % members},
            device_id_type=MESH,
        )

    for step in range(1, members):
        sum_copy(step).start()
    all_sums[member] = mine[...]
    for step in range(1, members):
        sum_copy(step).wait_send()
        sum_copy(step).wait_recv()

    coarse = all_sums[...].reshape(members * 2 * NB, 128)
    lane = lax.broadcasted_iota(jnp.int32, (8 * NB, 128), 1)
    total = jnp.zeros((8 * NB, 128), jnp.float32)
    for c in range(4):
        product = jnp.dot(
            inverse[c], coarse, precision=HIGHEST, preferred_element_type=jnp.float32
        )
        total = total + jnp.where(lane == c, product, 0.0)
    column = jnp.sum(total, axis=1, keepdims=True)
    place = lax.broadcasted_iota(jnp.int32, (8 * NB, FACE), 0)
    cell = cell_of(lax.broadcasted_iota(jnp.int32, (8 * NB, FACE), 1))
    spread = jnp.where(place % 4 == cell, column, 0.0)
    rows_of = lax.broadcasted_iota(jnp.int32, (2 * NB, 8 * NB), 1) // 4
    pick = (rows_of == lax.broadcasted_iota(jnp.int32, (2 * NB, 8 * NB), 0)).astype(jnp.float32)
    lifted = jnp.dot(pick, spread, precision=HIGHEST, preferred_element_type=jnp.float32)
    for b in range(NB):
        for half in (0, 1):
            part = slice(16 * half, 16 * half + 16)
            row = 2 * b + half
            out_ref[b, part, :] = u_ref[b, part, :] + lifted[row : row + 1, :]

    @pl.when(has_next)
    def _():
        for i in order:
            moves[i].wait_send()


def local(old_ids, field_old, source_old, kappa_old, refine, neighbors, coarse_inverse):
    members = lax.axis_size("member")
    devices = lax.axis_size(AXES)
    inverse = coarse_inverse[0].reshape(8 * NB, members * 2 * NB, 4).transpose(2, 0, 1)
    whole = (NB, EDGE, FACE)
    shapes = [field_old.shape] * 3 + [whole] * 9
    padded = (NB, 48, FACE + 256)
    shapes += [padded, whole, padded, whole, (NB, 6, EDGE, FACE), (2 * NB, 8, FACE)]
    shapes += [(2 * NB, 128), (members, 2 * NB, 128)]
    shapes += [(2,) + s for _ in range(8) for s in FACE_SHAPES]
    dma = pltpu.SemaphoreType.DMA
    scratch = [pltpu.VMEM(s, jnp.float32) for s in shapes]
    scratch += [dma((3,)), dma((3,)), dma((3,)), dma((4, 6)), dma((4, 6))]
    scratch += [dma((members,)), dma((members,))]
    return pl.pallas_call(
        functools.partial(main_kernel, members, devices),
        out_shape=jax.ShapeDtypeStruct(whole, jnp.float32),
        in_specs=[SM, SM, SM, VM, ANY, ANY, ANY],
        out_specs=VM,
        scratch_shapes=scratch,
        compiler_params=pltpu.CompilerParams(
            collective_id=1, has_side_effects=True, vmem_limit_bytes=VMEM_LIMIT
        ),
    )(old_ids, neighbors, refine, inverse, field_old, source_old, kappa_old)


def solution(mesh):
    in_specs = (
        P(AXES),
        P(AXES, None, None),
        P(AXES, None, None),
        P(AXES, None, None),
        P(AXES),
        P(AXES, None),
        P("group", "member", None),
    )
    return jax.shard_map(
        local, mesh=mesh, in_specs=in_specs, out_specs=P(AXES, None, None), check_vma=False
    )
```

```python
import functools

import jax
import jax.numpy as jnp
from jax import lax
from jax.experimental import pallas as pl
from jax.experimental.pallas import tpu as pltpu
from jax.sharding import PartitionSpec as P

OMEGA = 0.8
AXES = ("group", "member")
NB, EDGE, FACE = 8, 32, 1024
HIGHEST = lax.Precision.HIGHEST
VMEM_LIMIT = 56 * 2**20
VM = pl.BlockSpec(memory_space=pltpu.VMEM)
ANY = pl.BlockSpec(memory_space=pl.ANY)
MESH = pl.DeviceIdType.MESH
SM = pl.BlockSpec(memory_space=pltpu.SMEM)
FACE_SHAPES = ((4, FACE), (EDGE, 128), (8, FACE))


def roll(value, steps):
    width = value.shape[-1]
    return pltpu.roll(value, steps % width, value.ndim - 1)


def depth_lanes(shape):
    return lax.broadcasted_iota(jnp.int32, shape, len(shape) - 1) % EDGE


def blocks_of(axis, side):
    return [b for b in range(NB) if (b >> axis) % 2 == side]


def pack_faces(load, outs):
    segment = lax.broadcasted_iota(jnp.int32, (EDGE, 128), 1) // EDGE
    depth = depth_lanes((8, FACE))
    everything = slice(0, FACE)
    for side in (0, 1):
        for j, b in enumerate(blocks_of(0, side)):
            row = (EDGE - 1) * side
            outs[0][side][j : j + 1, :] = load(b, slice(row, row + 1), everything)
        packed = jnp.zeros((EDGE, 128), jnp.float32)
        for j, b in enumerate(blocks_of(1, side)):
            low = (FACE - 128) * side
            piece = load(b, slice(0, EDGE), slice(low, low + 128))
            packed = jnp.where(segment == j, roll(piece, EDGE * (j - 3 * side)), packed)
        outs[1][side][...] = packed
        packed = jnp.zeros((8, FACE), jnp.float32)
        for j, b in enumerate(blocks_of(2, side)):
            for part in range(4):
                slot = 4 * j + part
                piece = load(b, slice(8 * part, 8 * part + 8), everything)
                packed = jnp.where(depth == slot, roll(piece, slot - 31 * side), packed)
        outs[2][side][...] = packed


def fill(values, ghosts, nbrs, pad, sheet, mirror):
    everything = slice(0, FACE)
    depth = depth_lanes((8, FACE))
    for b in range(NB):
        pad[b, 8:40, 128 : 128 + FACE] = values[b]
        for side in (0, 1):
            inside = [(b >> axis) % 2 != side for axis in range(3)]
            has = [nbrs[b, 2 * axis + side] >= 0 for axis in range(3)]
            j = [blocks_of(a, side).index(b) if not inside[a] else 0 for a in range(3)]
            row, far = (EDGE - 1) * side, (EDGE - 1) * (1 - side)
            if inside[0]:
                ghost = values[b ^ 1, far : far + 1, :]
            else:
                ghost = ghosts[0][side][j[0] : j[0] + 1, :]
            spare = values[b, row : row + 1, :] if mirror else jnp.zeros_like(ghost)
            place = 7 + 33 * side
            pad[b, place : place + 1, 128 : 128 + FACE] = jnp.where(has[0], ghost, spare)
            low, high = (FACE - 128) * side, (FACE - 128) * (1 - side)
            if inside[1]:
                ghost = values[b ^ 2, :, high : high + 128]
            else:
                ghost = roll(ghosts[1][side][...], EDGE * (3 * (1 - side) - j[1]))
            if mirror:
                spare = roll(values[b, :, low : low + 128], EDGE * (3 - 6 * side))
            else:
                spare = jnp.zeros_like(ghost)
            place = (128 + FACE) * side
            pad[b, 8:40, place : place + 128] = jnp.where(has[1], ghost, spare)
        for part in range(4):
            rows = slice(8 * part, 8 * part + 8)
            own = values[b, rows, :]
            near = []
            for side in (0, 1):
                if (b >> 2) % 2 != side:
                    ghost = roll(values[b ^ 4, rows, :], 31 * (2 * side - 1))
                else:
                    slot = 4 * blocks_of(2, side).index(b) + part
                    ghost = roll(ghosts[2][side][...], 31 * side - slot)
                spare = own if mirror else jnp.zeros_like(own)
                near.append(jnp.where(nbrs[b, 4 + side] >= 0, ghost, spare))
            sheet[b, rows, :] = jnp.where(depth < EDGE // 2, near[0], near[1])


def across(pad, sheet, b, part):
    depth = depth_lanes((8, FACE))
    top = 8 + 8 * part
    inner = slice(128, 128 + FACE)
    x_minus = pad[b, top - 1 : top + 7, inner]
    x_plus = pad[b, top + 1 : top + 9, inner]
    whole = pad[b, top : top + 8, :]
    edge = sheet[b, 8 * part : 8 * part + 8, :]
    y_minus = roll(whole, EDGE)[:, inner]
    y_plus = roll(whole, -EDGE)[:, inner]
    z_minus = jnp.where(depth == 0, edge, roll(whole, 1)[:, inner])
    z_plus = jnp.where(depth == EDGE - 1, edge, roll(whole, -1)[:, inner])
    return whole[:, inner], (x_minus, x_plus, y_minus, y_plus, z_minus, z_plus)


def face_partners(members, devices):
    here = lax.axis_index("group") * members + lax.axis_index("member")
    nbits = devices.bit_length() - 1
    bits = [here // 2**i % 2 for i in range(nbits)]
    result = []
    for axis in range(3):
        own = [i for i in range(nbits) if i % 3 == axis]
        extent = 2 ** len(own)
        coord = sum(bits[i] * 2**n for n, i in enumerate(own))
        base = here - sum(bits[i] * 2**i for i in own)
        pair = []
        for step in (-1, 1):
            moved = coord + step
            inside = jnp.logical_and(moved >= 0, moved < extent)
            clipped = jnp.clip(moved, 0, extent - 1)
            index = base + sum(clipped // 2**n % 2 * 2**i for n, i in enumerate(own))
            pair.append((inside, (index // members, index % members)))
        result.append(pair)
    return result


def main_kernel(
    members, devices, old_ids, nbrs, refine, inverse, u_old, f_old, k_old, out_ref, low_ref, high_ref, *scratch
):
    olds, stages, gots = scratch[0:3], scratch[3:6], scratch[6:9]
    u_ref, f_ref, k_ref, pad_u, sheet_u, pad_k, sheet_k, weights, sums, mine, all_sums = scratch[9:20]
    sent, ghost = [], []
    for phase in range(4):
        base = 20 + 6 * phase
        sent.append([[r.at[0], r.at[1]] for r in scratch[base : base + 3]])
        ghost.append([[r.at[0], r.at[1]] for r in scratch[base + 3 : base + 6]])
    in_sem, move_send, move_recv, face_send, face_recv, sum_send, sum_recv = scratch[44:51]

    member = lax.axis_index("member")
    here = lax.axis_index("group") * members + member
    partners = face_partners(members, devices)
    has_next, has_prev = here < devices - 1, here > 0
    after = jnp.minimum(here + 1, devices - 1)
    before = jnp.maximum(here - 1, 0)
    after = (after // members, after % members)
    before = (before // members, before % members)

    order = (0, 2, 1)
    loads = [
        pltpu.make_async_copy(ref, olds[i], in_sem.at[i])
        for i, ref in enumerate((u_old, f_old, k_old))
    ]
    for i in order:
        loads[i].start()

    barrier = pltpu.get_barrier_semaphore()
    expected = has_next.astype(jnp.int32) + (members - 1)
    for axis in range(3):
        for side in (0, 1):
            inside, peer = partners[axis][side]
            expected = expected + inside.astype(jnp.int32)

            @pl.when(inside)
            def _():
                pl.semaphore_signal(barrier, inc=1, device_id=peer, device_id_type=MESH)

    for step in range(1, members):
        pl.semaphore_signal(
            barrier,
            inc=1,
            device_id={"member": (member + step) % members},
            device_id_type=MESH,
        )

    @pl.when(has_prev)
    def _():
        pl.semaphore_signal(barrier, inc=1, device_id=before, device_id_type=MESH)

    kept = jnp.int32(0)
    for slot in range(2 * NB):
        index = old_ids[slot]
        own = jnp.logical_and(index >= here * NB, index < here * NB + NB)
        kept = kept + own.astype(jnp.int32)
    kept = jnp.minimum(kept, NB)
    count = NB - kept

    moves = [
        pltpu.make_async_remote_copy(
            src_ref=stages[i],
            dst_ref=gots[i],
            send_sem=move_send.at[i],
            recv_sem=move_recv.at[i],
            device_id=after,
            device_id_type=MESH,
        )
        for i in range(3)
    ]
    for i in order:
        loads[i].wait()

        def stage(p, carry, i=i):
            stages[i][p] = olds[i][kept + p]
            return carry

        lax.fori_loop(0, NB, stage, 0)
        if i == 0:
            pl.semaphore_wait(barrier, expected)

        @pl.when(has_next)
        def _():
            moves[i].start()

    def settle(i, out):
        @pl.when(has_prev)
        def _():
            moves[i].wait_recv()

        def body(p, carry):
            out[p] = jnp.where(p < count, gots[i][p], olds[i][jnp.maximum(p - count, 0)])
            return carry

        lax.fori_loop(0, NB, body, 0)

    def face_copy(phase, axis, side, peer):
        return pltpu.make_async_remote_copy(
            src_ref=sent[phase][axis][side],
            dst_ref=ghost[phase][axis][1 - side],
            send_sem=face_send.at[phase, 2 * axis + side],
            recv_sem=face_recv.at[phase, 2 * axis + 1 - side],
            device_id=peer,
            device_id_type=MESH,
        )

    def send_faces(phase, values):
        pack_faces(lambda b, rows, lanes: values[b, rows, lanes], sent[phase])
        for axis in range(3):
            for side in (0, 1):
                inside, peer = partners[axis][side]

                @pl.when(inside)
                def _():
                    face_copy(phase, axis, side, peer).start()

    def take_faces(phase):
        for axis in range(3):
            for side in (0, 1):
                inside, peer = partners[axis][side]

                @pl.when(inside)
                def _():
                    face_copy(phase, axis, side, peer).wait_send()
                    face_copy(phase, axis, 1 - side, peer).wait_recv()

    settle(0, u_ref)
    send_faces(0, u_ref)
    settle(2, k_ref)
    send_faces(3, k_ref)
    take_faces(0)
    fill(u_ref, ghost[0], nbrs, pad_u, sheet_u, False)
    take_faces(3)
    fill(k_ref, ghost[3], nbrs, pad_k, sheet_k, True)

    def weigh(b, carry):
        half_scale = 0.5 + 0.5 * refine[b].astype(jnp.float32)
        for part in range(4):
            rows = slice(8 * part, 8 * part + 8)
            k, around = across(pad_k, sheet_k, b, part)
            for face in range(6):
                weights[b, face, rows, :] = half_scale * (k + around[face])
        return carry

    lax.fori_loop(0, NB, weigh, 0)
    settle(1, f_ref)

    def terms(b, part, with_diagonal):
        rows = slice(8 * part, 8 * part + 8)
        u, around = across(pad_u, sheet_u, b, part)
        applied = jnp.zeros_like(u)
        diagonal = jnp.zeros_like(u)
        for face in range(6):
            weight = weights[b, face, rows, :]
            applied = applied + weight * (u - around[face])
            if with_diagonal:
                diagonal = diagonal + weight
        return u, f_ref[b, rows, :] - applied, diagonal

    def sweep(b, carry):
        for part in range(4):
            u, gap, diagonal = terms(b, part, True)
            u_ref[b, 8 * part : 8 * part + 8, :] = u + OMEGA * gap / diagonal
        return carry

    for phase in (1, 2):
        lax.fori_loop(0, NB, sweep, 0)
        send_faces(phase, u_ref)
        take_faces(phase)
        fill(u_ref, ghost[phase], nbrs, pad_u, sheet_u, False)

    def residual(b, carry):
        for half in (0, 1):
            gap = terms(b, 2 * half, False)[1] + terms(b, 2 * half + 1, False)[1]
            sums[2 * b + half] = gap
        return carry

    lax.fori_loop(0, NB, residual, 0)

    def cell_of(lane):
        return lane // (FACE // 2) * 2 + lane % EDGE // (EDGE // 2)

    choose = cell_of(lax.broadcasted_iota(jnp.int32, (FACE, 128), 0)) == lax.broadcasted_iota(
        jnp.int32, (FACE, 128), 1
    )
    rows = jnp.sum(sums[...], axis=1)
    mine[...] = jnp.dot(
        rows, choose.astype(jnp.float32), precision=HIGHEST, preferred_element_type=jnp.float32
    ) * (EDGE // 2) ** (-1.5)

    def sum_copy(step):
        return pltpu.make_async_remote_copy(
            src_ref=mine,
            dst_ref=all_sums.at[member],
            send_sem=sum_send.at[step],
            recv_sem=sum_recv.at[step],
            device_id={"member": (member + step) % members},
            device_id_type=MESH,
        )

    for step in range(1, members):
        sum_copy(step).start()
    all_sums[member] = mine[...]
    for step in range(1, members):
        sum_copy(step).wait_send()
        sum_copy(step).wait_recv()

    coarse = all_sums[...].reshape(members * 2 * NB, 128)
    cells = members * 8 * NB
    lane = lax.broadcasted_iota(jnp.int32, (128, cells), 1) % 4
    copies = (lane == lax.broadcasted_iota(jnp.int32, (128, cells), 0)).astype(jnp.float32)
    repeated = jnp.dot(coarse, copies, precision=HIGHEST, preferred_element_type=jnp.float32)
    owner = lax.broadcasted_iota(jnp.int32, repeated.shape, 1) // 4
    chosen = owner == lax.broadcasted_iota(jnp.int32, repeated.shape, 0)
    vector = jnp.sum(jnp.where(chosen, repeated, 0.0), axis=0, keepdims=True)
    column = jnp.sum(inverse[0] * vector, axis=1, keepdims=True)
    place = lax.broadcasted_iota(jnp.int32, (8 * NB, FACE), 0)
    cell = cell_of(lax.broadcasted_iota(jnp.int32, (8 * NB, FACE), 1))
    spread = jnp.where(place % 4 == cell, column, 0.0)
    rows_of = lax.broadcasted_iota(jnp.int32, (NB, 8 * NB), 1) // 4
    for half, rows_ref in ((0, low_ref), (1, high_ref)):
        wanted = 2 * lax.broadcasted_iota(jnp.int32, (NB, 8 * NB), 0) + half
        pick = (rows_of == wanted).astype(jnp.float32)
        rows_ref[...] = jnp.dot(
            pick, spread, precision=HIGHEST, preferred_element_type=jnp.float32
        )
    out_ref[...] = u_ref[...]

    @pl.when(has_next)
    def _():
        for i in order:
            moves[i].wait_send()


def local(old_ids, field_old, source_old, kappa_old, refine, neighbors, coarse_inverse):
    members = lax.axis_size("member")
    devices = lax.axis_size(AXES)
    whole = (NB, EDGE, FACE)
    shapes = [field_old.shape] * 3 + [whole] * 9
    padded = (NB, 48, FACE + 256)
    shapes += [padded, whole, padded, whole, (NB, 6, EDGE, FACE), (2 * NB, 8, FACE)]
    shapes += [(2 * NB, 128), (members, 2 * NB, 128)]
    shapes += [(2,) + s for _ in range(8) for s in FACE_SHAPES]
    dma = pltpu.SemaphoreType.DMA
    scratch = [pltpu.VMEM(s, jnp.float32) for s in shapes]
    scratch += [dma((3,)), dma((3,)), dma((3,)), dma((4, 6)), dma((4, 6))]
    scratch += [dma((members,)), dma((members,))]
    u, low, high = pl.pallas_call(
        functools.partial(main_kernel, members, devices),
        out_shape=[
            jax.ShapeDtypeStruct(whole, jnp.float32),
            jax.ShapeDtypeStruct((NB, FACE), jnp.float32),
            jax.ShapeDtypeStruct((NB, FACE), jnp.float32),
        ],
        in_specs=[SM, SM, SM, VM, ANY, ANY, ANY],
        out_specs=[VM, VM, VM],
        scratch_shapes=scratch,
        compiler_params=pltpu.CompilerParams(
            collective_id=1, has_side_effects=True, vmem_limit_bytes=VMEM_LIMIT
        ),
    )(old_ids, neighbors, refine, coarse_inverse, field_old, source_old, kappa_old)
    half = lax.broadcasted_iota(jnp.int32, (1, EDGE, 1), 1) < EDGE // 2
    return u + jnp.where(half, low[:, None, :], high[:, None, :])


def solution(mesh):
    in_specs = (
        P(AXES),
        P(AXES, None, None),
        P(AXES, None, None),
        P(AXES, None, None),
        P(AXES),
        P(AXES, None),
        P("group", "member", None),
    )
    return jax.shard_map(
        local, mesh=mesh, in_specs=in_specs, out_specs=P(AXES, None, None), check_vma=False
    )
```

```python
import functools

import jax
import jax.numpy as jnp
from jax import lax
from jax.experimental import pallas as pl
from jax.experimental.pallas import tpu as pltpu
from jax.sharding import PartitionSpec as P

OMEGA = 0.8
AXES = ("group", "member")
NB, EDGE, FACE = 8, 32, 1024
HIGHEST = lax.Precision.HIGHEST
VMEM_LIMIT = 56 * 2**20
VM = pl.BlockSpec(memory_space=pltpu.VMEM)
ANY = pl.BlockSpec(memory_space=pl.ANY)
MESH = pl.DeviceIdType.MESH
SM = pl.BlockSpec(memory_space=pltpu.SMEM)
FACE_SHAPES = ((4, FACE), (EDGE, 128), (8, FACE))


def roll(value, steps):
    width = value.shape[-1]
    return pltpu.roll(value, steps % width, value.ndim - 1)


def depth_lanes(shape):
    return lax.broadcasted_iota(jnp.int32, shape, len(shape) - 1) % EDGE


def blocks_of(axis, side):
    return [b for b in range(NB) if (b >> axis) % 2 == side]


def pack_faces(load, outs):
    segment = lax.broadcasted_iota(jnp.int32, (EDGE, 128), 1) // EDGE
    depth = depth_lanes((8, FACE))
    everything = slice(0, FACE)
    for side in (0, 1):
        for j, b in enumerate(blocks_of(0, side)):
            row = (EDGE - 1) * side
            outs[0][side][j : j + 1, :] = load(b, slice(row, row + 1), everything)
        packed = jnp.zeros((EDGE, 128), jnp.float32)
        for j, b in enumerate(blocks_of(1, side)):
            low = (FACE - 128) * side
            piece = load(b, slice(0, EDGE), slice(low, low + 128))
            packed = jnp.where(segment == j, roll(piece, EDGE * (j - 3 * side)), packed)
        outs[1][side][...] = packed
        packed = jnp.zeros((8, FACE), jnp.float32)
        for j, b in enumerate(blocks_of(2, side)):
            for part in range(4):
                slot = 4 * j + part
                piece = load(b, slice(8 * part, 8 * part + 8), everything)
                packed = jnp.where(depth == slot, roll(piece, slot - 31 * side), packed)
        outs[2][side][...] = packed


def fill(values, ghosts, nbrs, pad, sheet, mirror):
    everything = slice(0, FACE)
    depth = depth_lanes((8, FACE))
    for b in range(NB):
        pad[b, 8:40, 128 : 128 + FACE] = values[b]
        for side in (0, 1):
            inside = [(b >> axis) % 2 != side for axis in range(3)]
            has = [nbrs[b, 2 * axis + side] >= 0 for axis in range(3)]
            j = [blocks_of(a, side).index(b) if not inside[a] else 0 for a in range(3)]
            row, far = (EDGE - 1) * side, (EDGE - 1) * (1 - side)
            if inside[0]:
                ghost = values[b ^ 1, far : far + 1, :]
            else:
                ghost = ghosts[0][side][j[0] : j[0] + 1, :]
            spare = values[b, row : row + 1, :] if mirror else jnp.zeros_like(ghost)
            place = 7 + 33 * side
            pad[b, place : place + 1, 128 : 128 + FACE] = jnp.where(has[0], ghost, spare)
            low, high = (FACE - 128) * side, (FACE - 128) * (1 - side)
            if inside[1]:
                ghost = values[b ^ 2, :, high : high + 128]
            else:
                ghost = roll(ghosts[1][side][...], EDGE * (3 * (1 - side) - j[1]))
            if mirror:
                spare = roll(values[b, :, low : low + 128], EDGE * (3 - 6 * side))
            else:
                spare = jnp.zeros_like(ghost)
            place = (128 + FACE) * side
            pad[b, 8:40, place : place + 128] = jnp.where(has[1], ghost, spare)
        for part in range(4):
            rows = slice(8 * part, 8 * part + 8)
            own = values[b, rows, :]
            near = []
            for side in (0, 1):
                if (b >> 2) % 2 != side:
                    ghost = roll(values[b ^ 4, rows, :], 31 * (2 * side - 1))
                else:
                    slot = 4 * blocks_of(2, side).index(b) + part
                    ghost = roll(ghosts[2][side][...], 31 * side - slot)
                spare = own if mirror else jnp.zeros_like(own)
                near.append(jnp.where(nbrs[b, 4 + side] >= 0, ghost, spare))
            sheet[b, rows, :] = jnp.where(depth < EDGE // 2, near[0], near[1])


def across(pad, sheet, b, part):
    depth = depth_lanes((8, FACE))
    top = 8 + 8 * part
    inner = slice(128, 128 + FACE)
    x_minus = pad[b, top - 1 : top + 7, inner]
    x_plus = pad[b, top + 1 : top + 9, inner]
    whole = pad[b, top : top + 8, :]
    edge = sheet[b, 8 * part : 8 * part + 8, :]
    y_minus = roll(whole, EDGE)[:, inner]
    y_plus = roll(whole, -EDGE)[:, inner]
    z_minus = jnp.where(depth == 0, edge, roll(whole, 1)[:, inner])
    z_plus = jnp.where(depth == EDGE - 1, edge, roll(whole, -1)[:, inner])
    return whole[:, inner], (x_minus, x_plus, y_minus, y_plus, z_minus, z_plus)


def face_partners(members, devices):
    here = lax.axis_index("group") * members + lax.axis_index("member")
    nbits = devices.bit_length() - 1
    bits = [here // 2**i % 2 for i in range(nbits)]
    result = []
    for axis in range(3):
        own = [i for i in range(nbits) if i % 3 == axis]
        extent = 2 ** len(own)
        coord = sum(bits[i] * 2**n for n, i in enumerate(own))
        base = here - sum(bits[i] * 2**i for i in own)
        pair = []
        for step in (-1, 1):
            moved = coord + step
            inside = jnp.logical_and(moved >= 0, moved < extent)
            clipped = jnp.clip(moved, 0, extent - 1)
            index = base + sum(clipped // 2**n % 2 * 2**i for n, i in enumerate(own))
            pair.append((inside, (index // members, index % members)))
        result.append(pair)
    return result


def main_kernel(
    members, devices, old_ids, nbrs, refine, inverse, u_old, f_old, k_old, out_ref, low_ref, high_ref, *scratch
):
    olds, stages, gots = scratch[0:3], scratch[3:6], scratch[6:9]
    u_ref, f_ref, k_ref, pad_u, sheet_u, pad_k, sheet_k, weights, sums, mine, all_sums = scratch[9:20]
    sent, ghost = [], []
    for phase in range(4):
        base = 20 + 6 * phase
        sent.append([[r.at[0], r.at[1]] for r in scratch[base : base + 3]])
        ghost.append([[r.at[0], r.at[1]] for r in scratch[base + 3 : base + 6]])
    in_sem, move_send, move_recv, face_send, face_recv, sum_send, sum_recv = scratch[44:51]

    member = lax.axis_index("member")
    here = lax.axis_index("group") * members + member
    partners = face_partners(members, devices)
    has_next, has_prev = here < devices - 1, here > 0
    after = jnp.minimum(here + 1, devices - 1)
    before = jnp.maximum(here - 1, 0)
    after = (after // members, after % members)
    before = (before // members, before % members)

    order = (0, 2, 1)
    loads = [
        pltpu.make_async_copy(ref, olds[i], in_sem.at[i])
        for i, ref in enumerate((u_old, f_old, k_old))
    ]
    for i in order:
        loads[i].start()

    barrier = pltpu.get_barrier_semaphore()
    expected = has_next.astype(jnp.int32) + (members - 1)
    for axis in range(3):
        for side in (0, 1):
            inside, peer = partners[axis][side]
            expected = expected + inside.astype(jnp.int32)

            @pl.when(inside)
            def _():
                pl.semaphore_signal(barrier, inc=1, device_id=peer, device_id_type=MESH)

    for step in range(1, members):
        pl.semaphore_signal(
            barrier,
            inc=1,
            device_id={"member": (member + step) % members},
            device_id_type=MESH,
        )

    @pl.when(has_prev)
    def _():
        pl.semaphore_signal(barrier, inc=1, device_id=before, device_id_type=MESH)

    kept = jnp.int32(0)
    for slot in range(2 * NB):
        index = old_ids[slot]
        own = jnp.logical_and(index >= here * NB, index < here * NB + NB)
        kept = kept + own.astype(jnp.int32)
    kept = jnp.minimum(kept, NB)
    count = NB - kept

    moves = [
        pltpu.make_async_remote_copy(
            src_ref=stages[i],
            dst_ref=gots[i],
            send_sem=move_send.at[i],
            recv_sem=move_recv.at[i],
            device_id=after,
            device_id_type=MESH,
        )
        for i in range(3)
    ]
    for i in order:
        loads[i].wait()

        def stage(p, carry, i=i):
            stages[i][p] = olds[i][kept + p]
            return carry

        lax.fori_loop(0, NB, stage, 0)
        if i == 0:
            pl.semaphore_wait(barrier, expected)

        @pl.when(has_next)
        def _():
            if i == 1:
                moves[0].wait_send()
                moves[2].wait_send()
            moves[i].start()

    def settle(i, out):
        @pl.when(has_prev)
        def _():
            moves[i].wait_recv()

        def body(p, carry):
            out[p] = jnp.where(p < count, gots[i][p], olds[i][jnp.maximum(p - count, 0)])
            return carry

        lax.fori_loop(0, NB, body, 0)

    def face_copy(phase, axis, side, peer):
        return pltpu.make_async_remote_copy(
            src_ref=sent[phase][axis][side],
            dst_ref=ghost[phase][axis][1 - side],
            send_sem=face_send.at[phase, 2 * axis + side],
            recv_sem=face_recv.at[phase, 2 * axis + 1 - side],
            device_id=peer,
            device_id_type=MESH,
        )

    def send_faces(phase, values):
        pack_faces(lambda b, rows, lanes: values[b, rows, lanes], sent[phase])
        for axis in range(3):
            for side in (0, 1):
                inside, peer = partners[axis][side]

                @pl.when(inside)
                def _():
                    face_copy(phase, axis, side, peer).start()

    def take_faces(phase):
        for axis in range(3):
            for side in (0, 1):
                inside, peer = partners[axis][side]

                @pl.when(inside)
                def _():
                    face_copy(phase, axis, side, peer).wait_send()
                    face_copy(phase, axis, 1 - side, peer).wait_recv()

    settle(0, u_ref)
    send_faces(0, u_ref)
    settle(2, k_ref)
    send_faces(3, k_ref)
    take_faces(0)
    fill(u_ref, ghost[0], nbrs, pad_u, sheet_u, False)
    take_faces(3)
    fill(k_ref, ghost[3], nbrs, pad_k, sheet_k, True)

    def weigh(b, carry):
        half_scale = 0.5 + 0.5 * refine[b].astype(jnp.float32)
        for part in range(4):
            rows = slice(8 * part, 8 * part + 8)
            k, around = across(pad_k, sheet_k, b, part)
            for face in range(6):
                weights[b, face, rows, :] = half_scale * (k + around[face])
        return carry

    lax.fori_loop(0, NB, weigh, 0)
    settle(1, f_ref)

    def terms(b, part, with_diagonal):
        rows = slice(8 * part, 8 * part + 8)
        u, around = across(pad_u, sheet_u, b, part)
        applied = jnp.zeros_like(u)
        diagonal = jnp.zeros_like(u)
        for face in range(6):
            weight = weights[b, face, rows, :]
            applied = applied + weight * (u - around[face])
            if with_diagonal:
                diagonal = diagonal + weight
        return u, f_ref[b, rows, :] - applied, diagonal

    def sweep(b, carry):
        for part in range(4):
            u, gap, diagonal = terms(b, part, True)
            u_ref[b, 8 * part : 8 * part + 8, :] = u + OMEGA * gap / diagonal
        return carry

    for phase in (1, 2):
        lax.fori_loop(0, NB, sweep, 0)
        send_faces(phase, u_ref)
        take_faces(phase)
        fill(u_ref, ghost[phase], nbrs, pad_u, sheet_u, False)

    def residual(b, carry):
        for half in (0, 1):
            gap = terms(b, 2 * half, False)[1] + terms(b, 2 * half + 1, False)[1]
            sums[2 * b + half] = gap
        return carry

    lax.fori_loop(0, NB, residual, 0)

    def cell_of(lane):
        return lane // (FACE // 2) * 2 + lane % EDGE // (EDGE // 2)

    choose = cell_of(lax.broadcasted_iota(jnp.int32, (FACE, 128), 0)) == lax.broadcasted_iota(
        jnp.int32, (FACE, 128), 1
    )
    rows = jnp.sum(sums[...], axis=1)
    mine[...] = jnp.dot(
        rows, choose.astype(jnp.float32), precision=HIGHEST, preferred_element_type=jnp.float32
    ) * (EDGE // 2) ** (-1.5)

    def sum_copy(step):
        return pltpu.make_async_remote_copy(
            src_ref=mine,
            dst_ref=all_sums.at[member],
            send_sem=sum_send.at[step],
            recv_sem=sum_recv.at[step],
            device_id={"member": (member + step) % members},
            device_id_type=MESH,
        )

    for step in range(1, members):
        sum_copy(step).start()
    all_sums[member] = mine[...]
    for step in range(1, members):
        sum_copy(step).wait_send()
        sum_copy(step).wait_recv()

    coarse = all_sums[...].reshape(members * 2 * NB, 128)
    cells = members * 8 * NB
    lane = lax.broadcasted_iota(jnp.int32, (128, cells), 1) % 4
    copies = (lane == lax.broadcasted_iota(jnp.int32, (128, cells), 0)).astype(jnp.float32)
    repeated = jnp.dot(coarse, copies, precision=HIGHEST, preferred_element_type=jnp.float32)
    owner = lax.broadcasted_iota(jnp.int32, repeated.shape, 1) // 4
    chosen = owner == lax.broadcasted_iota(jnp.int32, repeated.shape, 0)
    vector = jnp.sum(jnp.where(chosen, repeated, 0.0), axis=0, keepdims=True)
    column = jnp.sum(inverse[0] * vector, axis=1, keepdims=True)
    place = lax.broadcasted_iota(jnp.int32, (8 * NB, FACE), 0)
    cell = cell_of(lax.broadcasted_iota(jnp.int32, (8 * NB, FACE), 1))
    spread = jnp.where(place % 4 == cell, column, 0.0)
    rows_of = lax.broadcasted_iota(jnp.int32, (NB, 8 * NB), 1) // 4
    for half, rows_ref in ((0, low_ref), (1, high_ref)):
        wanted = 2 * lax.broadcasted_iota(jnp.int32, (NB, 8 * NB), 0) + half
        pick = (rows_of == wanted).astype(jnp.float32)
        rows_ref[...] = jnp.dot(
            pick, spread, precision=HIGHEST, preferred_element_type=jnp.float32
        )
    out_ref[...] = u_ref[...]

    @pl.when(has_next)
    def _():
        moves[1].wait_send()


def local(old_ids, field_old, source_old, kappa_old, refine, neighbors, coarse_inverse):
    members = lax.axis_size("member")
    devices = lax.axis_size(AXES)
    whole = (NB, EDGE, FACE)
    shapes = [field_old.shape] * 3 + [whole] * 9
    padded = (NB, 48, FACE + 256)
    shapes += [padded, whole, padded, whole, (NB, 6, EDGE, FACE), (2 * NB, 8, FACE)]
    shapes += [(2 * NB, 128), (members, 2 * NB, 128)]
    shapes += [(2,) + s for _ in range(8) for s in FACE_SHAPES]
    dma = pltpu.SemaphoreType.DMA
    scratch = [pltpu.VMEM(s, jnp.float32) for s in shapes]
    scratch += [dma((3,)), dma((3,)), dma((3,)), dma((4, 6)), dma((4, 6))]
    scratch += [dma((members,)), dma((members,))]
    u, low, high = pl.pallas_call(
        functools.partial(main_kernel, members, devices),
        out_shape=[
            jax.ShapeDtypeStruct(whole, jnp.float32),
            jax.ShapeDtypeStruct((NB, FACE), jnp.float32),
            jax.ShapeDtypeStruct((NB, FACE), jnp.float32),
        ],
        in_specs=[SM, SM, SM, VM, ANY, ANY, ANY],
        out_specs=[VM, VM, VM],
        scratch_shapes=scratch,
        compiler_params=pltpu.CompilerParams(
            collective_id=1, has_side_effects=True, vmem_limit_bytes=VMEM_LIMIT
        ),
    )(old_ids, neighbors, refine, coarse_inverse, field_old, source_old, kappa_old)
    half = lax.broadcasted_iota(jnp.int32, (1, EDGE, 1), 1) < EDGE // 2
    return u + jnp.where(half, low[:, None, :], high[:, None, :])


def solution(mesh):
    in_specs = (
        P(AXES),
        P(AXES, None, None),
        P(AXES, None, None),
        P(AXES, None, None),
        P(AXES),
        P(AXES, None),
        P("group", "member", None),
    )
    return jax.shard_map(
        local, mesh=mesh, in_specs=in_specs, out_specs=P(AXES, None, None), check_vma=False
    )
```

```python
import functools

import jax
import jax.numpy as jnp
from jax import lax
from jax.experimental import pallas as pl
from jax.experimental.pallas import tpu as pltpu
from jax.sharding import PartitionSpec as P

OMEGA = 0.8
AXES = ("group", "member")
NB, EDGE, FACE = 8, 32, 1024
HIGHEST = lax.Precision.HIGHEST
VMEM_LIMIT = 56 * 2**20
VM = pl.BlockSpec(memory_space=pltpu.VMEM)
ANY = pl.BlockSpec(memory_space=pl.ANY)
MESH = pl.DeviceIdType.MESH
SM = pl.BlockSpec(memory_space=pltpu.SMEM)
FACE_SHAPES = ((4, FACE), (EDGE, 128), (8, FACE))


def roll(value, steps):
    width = value.shape[-1]
    return pltpu.roll(value, steps % width, value.ndim - 1)


def depth_lanes(shape):
    return lax.broadcasted_iota(jnp.int32, shape, len(shape) - 1) % EDGE


def blocks_of(axis, side):
    return [b for b in range(NB) if (b >> axis) % 2 == side]


def pack_faces(load, outs):
    segment = lax.broadcasted_iota(jnp.int32, (EDGE, 128), 1) // EDGE
    depth = depth_lanes((8, FACE))
    everything = slice(0, FACE)
    for side in (0, 1):
        for j, b in enumerate(blocks_of(0, side)):
            row = (EDGE - 1) * side
            outs[0][side][j : j + 1, :] = load(b, slice(row, row + 1), everything)
        packed = jnp.zeros((EDGE, 128), jnp.float32)
        for j, b in enumerate(blocks_of(1, side)):
            low = (FACE - 128) * side
            piece = load(b, slice(0, EDGE), slice(low, low + 128))
            packed = jnp.where(segment == j, roll(piece, EDGE * (j - 3 * side)), packed)
        outs[1][side][...] = packed
        packed = jnp.zeros((8, FACE), jnp.float32)
        for j, b in enumerate(blocks_of(2, side)):
            for part in range(4):
                slot = 4 * j + part
                piece = load(b, slice(8 * part, 8 * part + 8), everything)
                packed = jnp.where(depth == slot, roll(piece, slot - 31 * side), packed)
        outs[2][side][...] = packed


def fill(values, ghosts, nbrs, pad, sheet, mirror):
    everything = slice(0, FACE)
    depth = depth_lanes((8, FACE))
    for b in range(NB):
        pad[b, 8:40, 128 : 128 + FACE] = values[b]
        for side in (0, 1):
            inside = [(b >> axis) % 2 != side for axis in range(3)]
            has = [nbrs[b, 2 * axis + side] >= 0 for axis in range(3)]
            j = [blocks_of(a, side).index(b) if not inside[a] else 0 for a in range(3)]
            row, far = (EDGE - 1) * side, (EDGE - 1) * (1 - side)
            if inside[0]:
                ghost = values[b ^ 1, far : far + 1, :]
            else:
                ghost = ghosts[0][side][j[0] : j[0] + 1, :]
            spare = values[b, row : row + 1, :] if mirror else jnp.zeros_like(ghost)
            place = 7 + 33 * side
            pad[b, place : place + 1, 128 : 128 + FACE] = jnp.where(has[0], ghost, spare)
            low, high = (FACE - 128) * side, (FACE - 128) * (1 - side)
            if inside[1]:
                ghost = values[b ^ 2, :, high : high + 128]
            else:
                ghost = roll(ghosts[1][side][...], EDGE * (3 * (1 - side) - j[1]))
            if mirror:
                spare = roll(values[b, :, low : low + 128], EDGE * (3 - 6 * side))
            else:
                spare = jnp.zeros_like(ghost)
            place = (128 + FACE) * side
            pad[b, 8:40, place : place + 128] = jnp.where(has[1], ghost, spare)
        for part in range(4):
            rows = slice(8 * part, 8 * part + 8)
            own = values[b, rows, :]
            near = []
            for side in (0, 1):
                if (b >> 2) % 2 != side:
                    ghost = roll(values[b ^ 4, rows, :], 31 * (2 * side - 1))
                else:
                    slot = 4 * blocks_of(2, side).index(b) + part
                    ghost = roll(ghosts[2][side][...], 31 * side - slot)
                spare = own if mirror else jnp.zeros_like(own)
                near.append(jnp.where(nbrs[b, 4 + side] >= 0, ghost, spare))
            sheet[b, rows, :] = jnp.where(depth < EDGE // 2, near[0], near[1])


def across(pad, sheet, b, part):
    depth = depth_lanes((8, FACE))
    top = 8 + 8 * part
    inner = slice(128, 128 + FACE)
    x_minus = pad[b, top - 1 : top + 7, inner]
    x_plus = pad[b, top + 1 : top + 9, inner]
    whole = pad[b, top : top + 8, :]
    edge = sheet[b, 8 * part : 8 * part + 8, :]
    y_minus = roll(whole, EDGE)[:, inner]
    y_plus = roll(whole, -EDGE)[:, inner]
    z_minus = jnp.where(depth == 0, edge, roll(whole, 1)[:, inner])
    z_plus = jnp.where(depth == EDGE - 1, edge, roll(whole, -1)[:, inner])
    return whole[:, inner], (x_minus, x_plus, y_minus, y_plus, z_minus, z_plus)


def face_partners(members, devices):
    here = lax.axis_index("group") * members + lax.axis_index("member")
    nbits = devices.bit_length() - 1
    bits = [here // 2**i % 2 for i in range(nbits)]
    result = []
    for axis in range(3):
        own = [i for i in range(nbits) if i % 3 == axis]
        extent = 2 ** len(own)
        coord = sum(bits[i] * 2**n for n, i in enumerate(own))
        base = here - sum(bits[i] * 2**i for i in own)
        pair = []
        for step in (-1, 1):
            moved = coord + step
            inside = jnp.logical_and(moved >= 0, moved < extent)
            clipped = jnp.clip(moved, 0, extent - 1)
            index = base + sum(clipped // 2**n % 2 * 2**i for n, i in enumerate(own))
            pair.append((inside, (index // members, index % members)))
        result.append(pair)
    return result


def main_kernel(
    members, devices, old_ids, nbrs, refine, inverse, u_old, f_old, k_old, out_ref, low_ref, high_ref, *scratch
):
    olds, stages, gots = scratch[0:3], scratch[3:6], scratch[6:9]
    u_ref, f_ref, k_ref, pad_u, sheet_u, pad_k, sheet_k, weights, sums, mine, all_sums = scratch[9:20]
    sent, ghost = [], []
    for phase in range(4):
        base = 20 + 6 * phase
        sent.append([[r.at[0], r.at[1]] for r in scratch[base : base + 3]])
        ghost.append([[r.at[0], r.at[1]] for r in scratch[base + 3 : base + 6]])
    in_sem, move_send, move_recv, face_send, face_recv, sum_send, sum_recv = scratch[44:51]

    member = lax.axis_index("member")
    here = lax.axis_index("group") * members + member
    partners = face_partners(members, devices)
    has_next, has_prev = here < devices - 1, here > 0
    after = jnp.minimum(here + 1, devices - 1)
    before = jnp.maximum(here - 1, 0)
    after = (after // members, after % members)
    before = (before // members, before % members)

    order = (0, 2, 1)
    loads = [
        pltpu.make_async_copy(ref, olds[i], in_sem.at[i])
        for i, ref in enumerate((u_old, f_old, k_old))
    ]
    for i in order:
        loads[i].start()

    barrier = pltpu.get_barrier_semaphore()
    expected = has_next.astype(jnp.int32) + (members - 1)
    for axis in range(3):
        for side in (0, 1):
            inside, peer = partners[axis][side]
            expected = expected + inside.astype(jnp.int32)

            @pl.when(inside)
            def _():
                pl.semaphore_signal(barrier, inc=1, device_id=peer, device_id_type=MESH)

    for step in range(1, members):
        pl.semaphore_signal(
            barrier,
            inc=1,
            device_id={"member": (member + step) % members},
            device_id_type=MESH,
        )

    @pl.when(has_prev)
    def _():
        pl.semaphore_signal(barrier, inc=1, device_id=before, device_id_type=MESH)

    kept = jnp.int32(0)
    for slot in range(2 * NB):
        index = old_ids[slot]
        own = jnp.logical_and(index >= here * NB, index < here * NB + NB)
        kept = kept + own.astype(jnp.int32)
    kept = jnp.minimum(kept, NB)
    count = NB - kept

    moves = [
        pltpu.make_async_remote_copy(
            src_ref=stages[i],
            dst_ref=gots[i],
            send_sem=move_send.at[i],
            recv_sem=move_recv.at[i],
            device_id=after,
            device_id_type=MESH,
        )
        for i in range(3)
    ]
    for i in order:
        loads[i].wait()

        def stage(p, carry, i=i):
            stages[i][p] = olds[i][kept + p]
            return carry

        lax.fori_loop(0, NB, stage, 0)
        if i == 0:
            pl.semaphore_wait(barrier, expected)

        @pl.when(has_next)
        def _():
            moves[i].start()

    def settle(i, out):
        @pl.when(has_prev)
        def _():
            moves[i].wait_recv()

        def body(p, carry):
            out[p] = jnp.where(p < count, gots[i][p], olds[i][jnp.maximum(p - count, 0)])
            return carry

        lax.fori_loop(0, NB, body, 0)

    def face_copy(phase, axis, side, peer):
        return pltpu.make_async_remote_copy(
            src_ref=sent[phase][axis][side],
            dst_ref=ghost[phase][axis][1 - side],
            send_sem=face_send.at[phase, 2 * axis + side],
            recv_sem=face_recv.at[phase, 2 * axis + 1 - side],
            device_id=peer,
            device_id_type=MESH,
        )

    def send_faces(phase, values):
        pack_faces(lambda b, rows, lanes: values[b, rows, lanes], sent[phase])
        for axis in range(3):
            for side in (0, 1):
                inside, peer = partners[axis][side]

                @pl.when(inside)
                def _():
                    face_copy(phase, axis, side, peer).start()

    def take_faces(phase):
        for axis in range(3):
            for side in (0, 1):
                inside, peer = partners[axis][side]

                @pl.when(inside)
                def _():
                    face_copy(phase, axis, side, peer).wait_send()
                    face_copy(phase, axis, 1 - side, peer).wait_recv()

    settle(0, u_ref)
    send_faces(0, u_ref)
    settle(2, k_ref)
    send_faces(3, k_ref)
    take_faces(0)
    fill(u_ref, ghost[0], nbrs, pad_u, sheet_u, False)
    take_faces(3)
    fill(k_ref, ghost[3], nbrs, pad_k, sheet_k, True)

    def weigh(b, carry):
        half_scale = 0.5 + 0.5 * refine[b].astype(jnp.float32)
        for part in range(4):
            rows = slice(8 * part, 8 * part + 8)
            k, around = across(pad_k, sheet_k, b, part)
            for face in range(6):
                weights[b, face, rows, :] = half_scale * (k + around[face])
        return carry

    lax.fori_loop(0, NB, weigh, 0)

    def terms(b, part, with_diagonal):
        rows = slice(8 * part, 8 * part + 8)
        u, around = across(pad_u, sheet_u, b, part)
        applied = jnp.zeros_like(u)
        diagonal = jnp.zeros_like(u)
        for face in range(6):
            weight = weights[b, face, rows, :]
            applied = applied + weight * (u - around[face])
            if with_diagonal:
                diagonal = diagonal + weight
        return u, applied, diagonal

    def sweep(b, carry):
        for part in range(4):
            rows = slice(8 * part, 8 * part + 8)
            u, applied, diagonal = terms(b, part, True)
            u_ref[b, rows, :] = u + OMEGA * (f_ref[b, rows, :] - applied) / diagonal
        return carry

    gain = gots[0]

    def early(b, carry):
        for part in range(4):
            rows = slice(8 * part, 8 * part + 8)
            u, applied, diagonal = terms(b, part, True)
            factor = OMEGA / diagonal
            gain[b, rows, :] = factor
            u_ref[b, rows, :] = u - factor * applied
        return carry

    def late(b, carry):
        u_ref[b] = u_ref[b] + gain[b] * f_ref[b]
        return carry

    lax.fori_loop(0, NB, early, 0)
    settle(1, f_ref)
    lax.fori_loop(0, NB, late, 0)

    for phase in (1, 2):
        if phase == 2:
            lax.fori_loop(0, NB, sweep, 0)
        send_faces(phase, u_ref)
        take_faces(phase)
        fill(u_ref, ghost[phase], nbrs, pad_u, sheet_u, False)

    def residual(b, carry):
        for half in (0, 1):
            gap = [
                f_ref[b, 8 * part : 8 * part + 8, :] - terms(b, part, False)[1]
                for part in (2 * half, 2 * half + 1)
            ]
            sums[2 * b + half] = gap[0] + gap[1]
        return carry

    lax.fori_loop(0, NB, residual, 0)

    def cell_of(lane):
        return lane // (FACE // 2) * 2 + lane % EDGE // (EDGE // 2)

    choose = cell_of(lax.broadcasted_iota(jnp.int32, (FACE, 128), 0)) == lax.broadcasted_iota(
        jnp.int32, (FACE, 128), 1
    )
    rows = jnp.sum(sums[...], axis=1)
    mine[...] = jnp.dot(
        rows, choose.astype(jnp.float32), precision=HIGHEST, preferred_element_type=jnp.float32
    ) * (EDGE // 2) ** (-1.5)

    def sum_copy(step):
        return pltpu.make_async_remote_copy(
            src_ref=mine,
            dst_ref=all_sums.at[member],
            send_sem=sum_send.at[step],
            recv_sem=sum_recv.at[step],
            device_id={"member": (member + step) % members},
            device_id_type=MESH,
        )

    for step in range(1, members):
        sum_copy(step).start()
    all_sums[member] = mine[...]
    for step in range(1, members):
        sum_copy(step).wait_send()
        sum_copy(step).wait_recv()

    coarse = all_sums[...].reshape(members * 2 * NB, 128)
    cells = members * 8 * NB
    lane = lax.broadcasted_iota(jnp.int32, (128, cells), 1) % 4
    copies = (lane == lax.broadcasted_iota(jnp.int32, (128, cells), 0)).astype(jnp.float32)
    repeated = jnp.dot(coarse, copies, precision=HIGHEST, preferred_element_type=jnp.float32)
    owner = lax.broadcasted_iota(jnp.int32, repeated.shape, 1) // 4
    chosen = owner == lax.broadcasted_iota(jnp.int32, repeated.shape, 0)
    vector = jnp.sum(jnp.where(chosen, repeated, 0.0), axis=0, keepdims=True)
    column = jnp.sum(inverse[0] * vector, axis=1, keepdims=True)
    place = lax.broadcasted_iota(jnp.int32, (8 * NB, FACE), 0)
    cell = cell_of(lax.broadcasted_iota(jnp.int32, (8 * NB, FACE), 1))
    spread = jnp.where(place % 4 == cell, column, 0.0)
    rows_of = lax.broadcasted_iota(jnp.int32, (NB, 8 * NB), 1) // 4
    for half, rows_ref in ((0, low_ref), (1, high_ref)):
        wanted = 2 * lax.broadcasted_iota(jnp.int32, (NB, 8 * NB), 0) + half
        pick = (rows_of == wanted).astype(jnp.float32)
        rows_ref[...] = jnp.dot(
            pick, spread, precision=HIGHEST, preferred_element_type=jnp.float32
        )
    out_ref[...] = u_ref[...]

    @pl.when(has_next)
    def _():
        for i in order:
            moves[i].wait_send()


def local(old_ids, field_old, source_old, kappa_old, refine, neighbors, coarse_inverse):
    members = lax.axis_size("member")
    devices = lax.axis_size(AXES)
    whole = (NB, EDGE, FACE)
    shapes = [field_old.shape] * 3 + [whole] * 9
    padded = (NB, 48, FACE + 256)
    shapes += [padded, whole, padded, whole, (NB, 6, EDGE, FACE), (2 * NB, 8, FACE)]
    shapes += [(2 * NB, 128), (members, 2 * NB, 128)]
    shapes += [(2,) + s for _ in range(8) for s in FACE_SHAPES]
    dma = pltpu.SemaphoreType.DMA
    scratch = [pltpu.VMEM(s, jnp.float32) for s in shapes]
    scratch += [dma((3,)), dma((3,)), dma((3,)), dma((4, 6)), dma((4, 6))]
    scratch += [dma((members,)), dma((members,))]
    u, low, high = pl.pallas_call(
        functools.partial(main_kernel, members, devices),
        out_shape=[
            jax.ShapeDtypeStruct(whole, jnp.float32),
            jax.ShapeDtypeStruct((NB, FACE), jnp.float32),
            jax.ShapeDtypeStruct((NB, FACE), jnp.float32),
        ],
        in_specs=[SM, SM, SM, VM, ANY, ANY, ANY],
        out_specs=[VM, VM, VM],
        scratch_shapes=scratch,
        compiler_params=pltpu.CompilerParams(
            collective_id=1, has_side_effects=True, vmem_limit_bytes=VMEM_LIMIT
        ),
    )(old_ids, neighbors, refine, coarse_inverse, field_old, source_old, kappa_old)
    half = lax.broadcasted_iota(jnp.int32, (1, EDGE, 1), 1) < EDGE // 2
    return u + jnp.where(half, low[:, None, :], high[:, None, :])


def solution(mesh):
    in_specs = (
        P(AXES),
        P(AXES, None, None),
        P(AXES, None, None),
        P(AXES, None, None),
        P(AXES),
        P(AXES, None),
        P("group", "member", None),
    )
    return jax.shard_map(
        local, mesh=mesh, in_specs=in_specs, out_specs=P(AXES, None, None), check_vma=False
    )
```
